32 devices in a mesh: section: 2 (over x), dp: 4 (over y, core), tensor: 4 (over z).
Axes of the slice: x: 2, y: 2, z: 4, core: 2. Of those that a mesh axis runs over, the one named last changes fastest.
Arguments:
- ends_in: bfloat16 [2, 4, 2048, 768], P('section', None, ('dp', 'tensor')), may hold values from -6 to 6
- segments: int32 [4, 4, 512], P(None, 'dp'), may hold values from 0 to 3, as said below
- qkv_weight: bfloat16 [2, 2304, 768], P('section', ('tensor', 'dp')), may hold values from -0.21875 to 0.21875
- qkv_bias: bfloat16 [2, 2, 768], P('section', None, ('tensor', 'dp')), may hold values from -1.5 to 1.5
- output_weight: bfloat16 [2, 768, 768], P('section', ('tensor', 'dp')), may hold values from -0.875 to 0.875
- expand_weight: bfloat16 [2, 3072, 768], P('section', ('tensor', 'dp')), may hold values from -0.21875 to 0.21875
- expand_bias: bfloat16 [2, 3072], P('section', ('tensor', 'dp')), may hold values from -1.5 to 1.5
- contract_weight: bfloat16 [2, 3072, 768], P('section', ('tensor', 'dp')), may hold values from -0.109375 to 0.109375
- norm_gains: bfloat16 [2, 2, 768], P('section', None, 'dp'), may hold values from 0.5 to 1.5
- row_biases: bfloat16 [2, 4, 768], P('section', None, 'dp'), may hold values from -1.5 to 1.5
Outputs:
- ends_out: float32 [2, 4, 2048, 768], P('section', None, ('dp', 'tensor'))
- qkv_weight_grad: float32 [2, 2304, 768], P('section', ('tensor', 'dp'))
- qkv_bias_grad: float32 [2, 2, 768], P('section', None, ('tensor', 'dp'))
- output_weight_grad: float32 [2, 768, 768], P('section', ('tensor', 'dp'))
- expand_weight_grad: float32 [2, 3072, 768], P('section', ('tensor', 'dp'))
- expand_bias_grad: float32 [2, 3072], P('section', ('tensor', 'dp'))
- contract_weight_grad: float32 [2, 3072, 768], P('section', ('tensor', 'dp'))
- norm_gains_grad: float32 [2, 2, 768], P('section', None, 'dp')
- row_biases_grad: float32 [2, 4, 768], P('section', None, 'dp')
The draws below stay inside these ranges and needn't reach their ends.
Inputs may be any that keep to these rules, and one draw needn't show every extreme that they name: `segments`: the sequences are consecutive cuts of one stream of documents in order (micro-batch, sequence); segment numbers count the documents met within a sequence from 0 and never fall along it.
All inputs are finite; a program needn't handle non-finite values.
Results may differ from the reference program's by a relative error of at most 0.03.
Values may be sent and summed in bfloat16 or wider, within the bound.
A program may use at most 128 MiB of HBM per device.

```python
import math
import jax
import jax.numpy as jnp
from jax import lax

D = 768
HEADS = 12
HD = 64
FF = 3072
LEN = 512
MB = 4
SEQ_DEV = 1
SEQS = 4
ROWS = 2048
LAYERS = 2
N_SECTION = 2
N_DP = 4


def draw_segments(key, part):
    key = jax.random.fold_in(key, 11)
    total = MB * SEQS * LEN
    shortest = max(2, LEN * 200 // 512)
    longest = LEN * 2000 // 512
    doc_count = total // shortest + 4
    length_key, start_key = jax.random.split(key)
    doc_lengths = jax.random.randint(length_key, (doc_count,), shortest, longest + 1, dtype=jnp.int32)
    first_piece = jax.random.randint(start_key, (), 1, max(2, LEN // 8) + 1, dtype=jnp.int32)
    doc_lengths = doc_lengths.at[0].set(first_piece)
    doc_lengths = doc_lengths.at[1].set(jnp.int32(shortest))
    doc_lengths = doc_lengths.at[2].set(jnp.int32(shortest))
    doc_lengths = doc_lengths.at[3].set(jnp.int32(longest))
    doc_ends = jnp.cumsum(doc_lengths).astype(jnp.int32)
    positions = jnp.arange(total, dtype=jnp.int32)
    doc_ids = jnp.searchsorted(doc_ends, positions, side='right').astype(jnp.int32)
    doc_ids = doc_ids.reshape(MB * SEQS, LEN)
    numbers = doc_ids - doc_ids[:, :1]
    return numbers.reshape(MB, SEQS, LEN).astype(jnp.int32)


def level_of(stream_key, dims, cuts, smallest, largest):
    level, own = 1.0, jax.random.fold_in(stream_key, 6)
    for axis_at, shards_of in cuts:
        draws = jnp.exp(jax.random.uniform(jax.random.fold_in(own, axis_at), (shards_of,), jnp.float32, smallest / len(cuts), largest / len(cuts)))
        level = level * jnp.repeat(draws, dims[axis_at] // shards_of).reshape([-1 if axis == axis_at else 1 for axis in range(len(dims))])
    return level


def gaussian(rng, dims, spread, reach, shards=(), kind=jnp.bfloat16):
    level = level_of(rng, dims, shards, -0.22, 0.18) if shards else 1.0
    drawn = jax.random.normal(rng, dims, jnp.float32) * spread * level
    return jnp.minimum(jnp.maximum(drawn, -reach), reach).astype(kind)


def setup_inputs(seed: int = 0) -> dict:
    splits = jax.random.split(jax.random.key(seed), 11)
    return {
        "ends_in": gaussian(splits[0], (2, MB, ROWS, D), 1.0, 6.0, ((0, 2), (2, 16))),
        "segments": draw_segments(jax.random.fold_in(splits[10], 71), 0),
        "qkv_weight": gaussian(splits[2], (LAYERS, 3 * D, D), D ** -0.5, 0.21875, ((0, 2), (1, 16))),
        "qkv_bias": gaussian(splits[3], (LAYERS, 2, D), 0.3, 1.5, ((0, 2), (2, 16))),
        "output_weight": gaussian(splits[4], (LAYERS, D, D), (D // 16) ** -0.5, 0.875, ((0, 2), (1, 16))),
        "expand_weight": gaussian(splits[5], (LAYERS, FF, D), D ** -0.5, 0.21875, ((0, 2), (1, 16))),
        "expand_bias": gaussian(splits[6], (LAYERS, FF), 0.3, 1.5, ((0, 2), (1, 16))),
        "contract_weight": gaussian(splits[7], (LAYERS, FF, D), FF ** -0.5, 0.109375, ((0, 2), (1, 16))),
        "norm_gains": jnp.clip(1.0 + 0.1 * jax.random.normal(splits[8], (LAYERS, 2, D), jnp.float32), 0.5, 1.5).astype(jnp.bfloat16),
        "row_biases": gaussian(splits[9], (LAYERS, 4, D), 0.3, 1.5, ((0, 2), (2, 4))),
    }


@jax.custom_vjp
def low(v):
    return lax.optimization_barrier(v.astype(jnp.bfloat16)).astype(jnp.float32)

@jax.custom_vjp
def low_back(v):
    return v

def low_keep(v):
    return (low(v), None)

def low_pass(kept, grad):
    return (grad,)

def back_keep(v):
    return (v, None)

def back_low(kept, grad):
    return (low(grad),)
low.defvjp(low_keep, low_pass)
low_back.defvjp(back_keep, back_low)
EPS = 1e-05
MASKED = -1e+30
HIGH = lax.Precision.HIGHEST

def norm_rows(hidden, gain_row, shift_row):
    average = lax.optimization_barrier(jnp.mean(hidden, axis=-1, keepdims=True))
    centred = hidden - average
    variance = lax.optimization_barrier(jnp.mean(centred * centred, axis=-1, keepdims=True))
    return centred * lax.rsqrt(variance + EPS) * gain_row + shift_row

def attend_sequence(block_pair):
    joined, segment_ids = block_pair
    query_parts = joined[:, :, 0]
    key_parts = joined[:, :, 1]
    value_parts = joined[:, :, 2]
    scores = jnp.einsum('qhe,khe->hqk', query_parts, key_parts, precision=HIGH) * HD ** (-0.5)
    scores = low_back(scores)
    same_segment = (segment_ids[:, None] == segment_ids[None, :])[None]
    masked_scores = jnp.where(same_segment, scores, MASKED)
    row_peak = lax.optimization_barrier(jnp.max(masked_scores, axis=-1, keepdims=True))
    exp_scores = jnp.where(same_segment, jnp.exp(masked_scores - row_peak), 0.0)
    soft_weights = low(exp_scores / lax.optimization_barrier(jnp.sum(exp_scores, axis=-1, keepdims=True)))
    return jnp.einsum('hqk,khe->qhe', soft_weights, value_parts, precision=HIGH)

def encoder_layer(inputs, segment_ids, weights):
    qkv_weight, qkv_bias, output_weight, expand_weight, expand_bias, contract_weight, norm_gains, row_biases = weights
    row_count = inputs.shape[0]
    mixed = jnp.dot(inputs, qkv_weight.T, precision=HIGH).reshape(row_count, HEADS, 3, HD)
    bias_parts = jnp.stack([qkv_bias[0].reshape(HEADS, HD), jnp.zeros((HEADS, HD), jnp.float32), qkv_bias[1].reshape(HEADS, HD)], axis=1)
    joined = low_back(low(mixed + bias_parts))
    context = lax.map(jax.checkpoint(attend_sequence), (joined.reshape(-1, LEN, HEADS, 3, HD), segment_ids))
    context = low_back(low(context.reshape(row_count, D)))
    attended = low_back(jnp.dot(context, output_weight, precision=HIGH))
    first = norm_rows(inputs + attended + row_biases[0], norm_gains[0], row_biases[1])
    pre_act = low_back(jnp.dot(low(first), expand_weight.T, precision=HIGH) + expand_bias)
    activated = low(jax.nn.gelu(pre_act, approximate=False))
    returned = low_back(jnp.dot(activated, contract_weight, precision=HIGH))
    return norm_rows(first + returned + row_biases[2], norm_gains[1], row_biases[3])

def stack_forward(inputs, weights_all, segment_ids):
    hidden = inputs
    for layer_index in range(N_SECTION):
        hidden = encoder_layer(hidden, segment_ids, tuple((item[layer_index] for item in weights_all)))
        hidden = low_back(low(hidden)) if layer_index + 1 < N_SECTION else low(hidden)
    return hidden

def reference(ends_in, segments, qkv_weight, qkv_bias, output_weight, expand_weight, expand_bias, contract_weight, norm_gains, row_biases):
    params = tuple((item.astype(jnp.float32) for item in (qkv_weight, qkv_bias, output_weight, expand_weight, expand_bias, contract_weight, norm_gains, row_biases)))
    group_seqs = SEQ_DEV * math.gcd(N_DP, 4)
    group_count = MB * SEQS // group_seqs
    inputs_all = ends_in[0].astype(jnp.float32).reshape(group_count, group_seqs * LEN, D)
    cotangents = ends_in[1].astype(jnp.float32).reshape(group_count, group_seqs * LEN, D)
    segment_groups = segments.reshape(group_count, group_seqs, LEN)

    def one_group(carry, group_items):
        inputs, cotangent, segment_ids = group_items
        output, pullback = jax.vjp(lambda first_arg, second_arg: stack_forward(first_arg, second_arg, segment_ids), inputs, params)
        input_grad, weight_grads = pullback(cotangent)
        summed = tuple((left_item + right_item for left_item, right_item in zip(carry, weight_grads)))
        return (summed, (input_grad, output))
    zero_grads = tuple((jnp.zeros_like(item) for item in params))
    grads, (input_grads, outputs) = lax.scan(one_group, zero_grads, (inputs_all, cotangents, segment_groups))
    ends_out = jnp.stack([input_grads.reshape(MB, ROWS, D), outputs.reshape(MB, ROWS, D)])
    return (ends_out, grads[0], grads[1], grads[2], grads[3], grads[4], grads[5], grads[6], grads[7])
```

```python
import jax
import jax.numpy as jnp
from jax import lax
from jax.sharding import PartitionSpec as P

HD = 64
EPS = 1e-05
MASKED = -1e30
F32 = jnp.float32
BF16 = jnp.bfloat16
SHARDS = ("tensor", "dp")


def rows_by_units(left_side, right_side):
    return lax.dot_general(
        left_side, right_side, (((1,), (1,)), ((), ())), preferred_element_type=F32
    )


def over_rows(left_side, right_side):
    return lax.dot_general(
        left_side, right_side, (((0,), (0,)), ((), ())), preferred_element_type=F32
    )


def plain(left_side, right_side):
    return jnp.dot(left_side, right_side, preferred_element_type=F32)


def norm_forward(hidden, gain_row, shift_row):
    average = jnp.mean(hidden, axis=-1, keepdims=True)
    centred = hidden - average
    variance = jnp.mean(centred * centred, axis=-1, keepdims=True)
    inverse = lax.rsqrt(variance + EPS)
    normed = centred * inverse
    return (normed * gain_row + shift_row, normed, inverse)


def norm_backward(grad_out, normed, inverse, gain_row):
    grad_normed = grad_out * gain_row
    inner_sum = jnp.mean(grad_normed, axis=-1, keepdims=True)
    along_norm = jnp.mean(grad_normed * normed, axis=-1, keepdims=True)
    return inverse * (grad_normed - inner_sum - normed * along_norm)


def attend(joined, segment_ids):
    parts = joined.reshape(joined.shape[0], -1, 3, HD)
    query, key, value = parts[:, :, 0], parts[:, :, 1], parts[:, :, 2]
    scores = jnp.einsum("qhe,khe->hqk", query, key, preferred_element_type=F32) * HD ** (-0.5)
    same = (segment_ids[:, None] == segment_ids[None, :])[None]
    scores = jnp.where(same, scores, MASKED)
    peak = jnp.max(scores, axis=-1, keepdims=True)
    powers = jnp.exp(scores - peak)
    total = jnp.sum(powers, axis=-1, keepdims=True)
    soft = (powers / total).astype(BF16)
    context = jnp.einsum("hqk,khe->qhe", soft, value, preferred_element_type=F32)
    return (context.reshape(joined.shape[0], -1).astype(BF16), soft)


def attend_back(joined, soft, grad_context):
    parts = joined.reshape(joined.shape[0], -1, 3, HD)
    query, key, value = parts[:, :, 0], parts[:, :, 1], parts[:, :, 2]
    grad_heads = grad_context.reshape(value.shape)
    grad_value = jnp.einsum("hqk,qhe->khe", soft, grad_heads, preferred_element_type=F32)
    grad_soft = jnp.einsum("qhe,khe->hqk", grad_heads, value, preferred_element_type=F32)
    soft_float = soft.astype(F32)
    inner_sum = jnp.sum(grad_soft * soft_float, axis=-1, keepdims=True)
    grad_scores = (soft_float * (grad_soft - inner_sum)).astype(BF16)
    grad_query = jnp.einsum("hqk,khe->qhe", grad_scores, key, preferred_element_type=F32)
    grad_key = jnp.einsum("hqk,qhe->khe", grad_scores, query, preferred_element_type=F32)
    scale = HD ** (-0.5)
    stacked = jnp.stack([grad_query * scale, grad_key * scale, grad_value], axis=2)
    return stacked.reshape(joined.shape).astype(BF16)


def gelu_pair(pre_act):
    cdf = 0.5 * (1.0 + lax.erf(pre_act * 0.5**0.5))
    density = jnp.exp(-0.5 * pre_act * pre_act) * 0.3989422804014327
    return (pre_act * cdf, cdf + pre_act * density)


def layer_forward(inputs, segment_ids, weights, smalls):
    qkv, output, expand, contract = weights
    qkv_bias, expand_bias, gains, biases = smalls
    joined = (rows_by_units(inputs, qkv) + qkv_bias).astype(BF16)
    context, soft = attend(joined, segment_ids)
    hidden_one = inputs.astype(F32) + plain(context, output) + biases[0]
    first, normed_one, inverse_one = norm_forward(hidden_one, gains[0], biases[1])
    mid_rows = first.astype(BF16)
    pre_act = rows_by_units(mid_rows, expand) + expand_bias
    activated, slope = gelu_pair(pre_act)
    activated = activated.astype(BF16)
    hidden_two = first + plain(activated, contract) + biases[2]
    result, normed_two, inverse_two = norm_forward(hidden_two, gains[1], biases[3])
    saved = (
        joined,
        soft,
        context,
        normed_one,
        inverse_one,
        mid_rows,
        activated,
        slope.astype(BF16),
        normed_two,
        inverse_two,
    )
    return (result.astype(BF16), saved)


def layer_backward(grad_result, weights, gains, saved):
    qkv, output, expand, contract = weights
    joined, soft, context, normed_one, inverse_one, mid_rows, activated, slope, normed_two, inverse_two = saved
    grad_result = grad_result.astype(F32)
    grad_two = norm_backward(grad_result, normed_two, inverse_two, gains[1])
    grad_returned = grad_two.astype(BF16)
    grad_pre = (rows_by_units(grad_returned, contract) * slope.astype(F32)).astype(BF16)
    grad_first = grad_two + plain(grad_pre, expand)
    grad_one = norm_backward(grad_first, normed_one, inverse_one, gains[0])
    grad_attended = grad_one.astype(BF16)
    grad_context = rows_by_units(grad_attended, output).astype(BF16)
    grad_joined = attend_back(joined, soft, grad_context)
    grad_inputs = grad_one + plain(grad_joined, qkv)
    return (
        grad_inputs.astype(BF16),
        (grad_result, grad_two, grad_returned, grad_pre, grad_first, grad_one, grad_attended, grad_joined),
    )


def weight_scatter(grad):
    return lax.psum_scatter(grad.astype(BF16), SHARDS, scatter_dimension=0, tiled=True).astype(F32)


def shards(
    ends_in,
    segments,
    qkv_weight,
    qkv_bias,
    output_weight,
    expand_weight,
    expand_bias,
    contract_weight,
    norm_gains,
    row_biases,
):
    section = lax.axis_index("section")
    along = lax.axis_index("tensor")
    dp_at = lax.axis_index("dp")
    dp_count = lax.axis_size("dp")
    tensor_count = lax.axis_size("tensor")
    flat_count = dp_count * tensor_count
    features = ends_in.shape[-1]
    heads = features // HD
    bias_part = qkv_bias.shape[-1]
    unit_part = expand_bias.shape[-1]
    norm_part = norm_gains.shape[-1]

    own = lax.all_to_all(ends_in[0], "tensor", 0, 1, tiled=True)[0]
    packed = jnp.concatenate(
        [qkv_bias[0].reshape(-1), expand_bias[0], norm_gains[0].reshape(-1), row_biases[0].reshape(-1)]
    )
    packed = lax.all_gather(packed, SHARDS, axis=0, tiled=False).astype(F32)
    weights = tuple(
        lax.all_gather(item[0], SHARDS, axis=0, tiled=True)
        for item in (qkv_weight, output_weight, expand_weight, contract_weight)
    )
    cut_one = 2 * bias_part
    cut_two = cut_one + unit_part
    cut_three = cut_two + 2 * norm_part
    biases_qv = packed[:, :cut_one].reshape(flat_count, 2, bias_part).transpose(1, 0, 2).reshape(2, heads, HD)
    qkv_bias_row = jnp.stack(
        [biases_qv[0], jnp.zeros((heads, HD), F32), biases_qv[1]], axis=1
    ).reshape(-1)
    expand_bias_row = packed[:, cut_one:cut_two].reshape(-1)
    gains = packed[:dp_count, cut_two:cut_three].reshape(dp_count, 2, norm_part).transpose(1, 0, 2).reshape(2, features)
    biases = packed[:dp_count, cut_three:].reshape(dp_count, 4, norm_part).transpose(1, 0, 2).reshape(4, features)
    smalls = (qkv_bias_row, expand_bias_row, gains, biases)
    segment_ids = lax.dynamic_index_in_dim(segments, along, 0, keepdims=False)[0]

    early_result, _ = layer_forward(own, segment_ids, weights, smalls)
    arriving = lax.ppermute(early_result, "section", [(0, 1)])
    inputs = jnp.where(section == 0, own, arriving)
    result, saved = layer_forward(inputs, segment_ids, weights, smalls)
    early_grad, _ = layer_backward(own, weights, gains, saved)
    arriving_grad = lax.ppermute(early_grad, "section", [(1, 0)])
    cotangent = jnp.where(section == 1, own, arriving_grad)
    grad_inputs, items = layer_backward(cotangent, weights, gains, saved)
    grad_result, grad_two, grad_returned, grad_pre, grad_first, grad_one, grad_attended, grad_joined = items
    joined, soft, context, normed_one, inverse_one, mid_rows, activated, slope, normed_two, inverse_two = saved

    contract_grad = weight_scatter(over_rows(activated, grad_returned))
    expand_grad = weight_scatter(over_rows(grad_pre, mid_rows))
    output_grad = weight_scatter(over_rows(context, grad_attended))
    qkv_grad = weight_scatter(over_rows(grad_joined, inputs))
    joined_sums = jnp.sum(grad_joined.astype(F32), axis=0).reshape(heads, 3, HD)
    small_grads = jnp.concatenate(
        [
            joined_sums[:, 0].reshape(-1),
            joined_sums[:, 2].reshape(-1),
            jnp.sum(grad_first * normed_one, axis=0),
            jnp.sum(grad_result * normed_two, axis=0),
            jnp.sum(grad_one, axis=0),
            jnp.sum(grad_first, axis=0),
            jnp.sum(grad_two, axis=0),
            jnp.sum(grad_result, axis=0),
            jnp.sum(grad_pre.astype(F32), axis=0),
        ]
    )
    small_sums = lax.psum(small_grads, SHARDS)
    flat_at = along * dp_count + dp_at
    table = small_sums[: 8 * features].reshape(8, features)
    qkv_bias_grad = lax.dynamic_slice_in_dim(table[:2], flat_at * bias_part, bias_part, 1)
    norm_grads = lax.dynamic_slice_in_dim(table[2:], dp_at * norm_part, norm_part, 1)
    expand_bias_grad = lax.dynamic_slice_in_dim(
        small_sums[8 * features :], flat_at * unit_part, unit_part, 0
    )
    ends = jnp.where(section == 0, grad_inputs, result).reshape(ends_in.shape[1:])
    ends_out = lax.all_to_all(ends, "tensor", 0, 0, tiled=True).astype(F32)
    return (
        ends_out[None],
        qkv_grad[None],
        qkv_bias_grad[None],
        output_grad[None],
        expand_grad[None],
        expand_bias_grad[None],
        contract_grad[None],
        norm_grads[:2][None],
        norm_grads[2:][None],
    )


def solution(mesh):
    rows = P("section", None, ("dp", "tensor"), None)
    units = P("section", SHARDS, None)
    biases = P("section", None, SHARDS)
    norms = P("section", None, "dp")
    vector = P("section", SHARDS)
    return jax.shard_map(
        shards,
        mesh=mesh,
        in_specs=(rows, P(None, "dp", None), units, biases, units, units, vector, units, norms, norms),
        out_specs=(rows, units, biases, units, units, vector, units, norms, norms),
        check_vma=False,
    )
```

```python
from functools import partial

import jax
import jax.numpy as jnp
from jax import lax
from jax.experimental import pallas as pl
from jax.experimental.pallas import tpu as pltpu
from jax.sharding import PartitionSpec as P

HD = 64
EPS = 1e-05
MASKED = -1e30
F32 = jnp.float32
BF16 = jnp.bfloat16
SHARDS = ("tensor", "dp")


def rows_by_units(left_side, right_side):
    return lax.dot_general(
        left_side, right_side, (((1,), (1,)), ((), ())), preferred_element_type=F32
    )


def over_rows(left_side, right_side):
    return lax.dot_general(
        left_side, right_side, (((0,), (0,)), ((), ())), preferred_element_type=F32
    )


def plain(left_side, right_side):
    return jnp.dot(left_side, right_side, preferred_element_type=F32)


def norm_forward(hidden, gain_row, shift_row):
    average = jnp.mean(hidden, axis=-1, keepdims=True)
    centred = hidden - average
    variance = jnp.mean(centred * centred, axis=-1, keepdims=True)
    inverse = lax.rsqrt(variance + EPS)
    normed = centred * inverse
    return (normed * gain_row + shift_row, normed, inverse)


def norm_backward(grad_out, normed, inverse, gain_row):
    grad_normed = grad_out * gain_row
    inner_sum = jnp.mean(grad_normed, axis=-1, keepdims=True)
    along_norm = jnp.mean(grad_normed * normed, axis=-1, keepdims=True)
    return inverse * (grad_normed - inner_sum - normed * along_norm)


SCALE = HD ** (-0.5)
PAIR = 2 * HD
CHUNK = 768
VMEM_BYTES = 50 * 1024 * 1024


def head_part(block, head, part):
    at = (head * 3 + part) * HD
    return block[:, at : at + HD]


def attention_kernel(
    keep, x_ref, qkv_ref, qkv_bias_ref, column_ref, row_ref, output_ref, gains_ref, biases_ref, *rest
):
    if keep:
        first_ref, joined_ref, soft_ref, context_ref, normed_ref, inverse_ref, total = rest
    else:
        first_ref, total = rest
    step = pl.program_id(0)
    joined = (rows_by_units(x_ref[...], qkv_ref[...]) + qkv_bias_ref[0]).astype(BF16)
    same = column_ref[...] == row_ref[...]
    contexts = []
    for head in range(2):
        query = head_part(joined, head, 0) * jnp.asarray(SCALE, BF16)
        scores = jnp.where(same, rows_by_units(query, head_part(joined, head, 1)), MASKED)
        powers = jnp.exp(scores - jnp.max(scores, axis=-1, keepdims=True))
        soft = (powers * (1.0 / jnp.sum(powers, axis=-1, keepdims=True))).astype(BF16)
        contexts.append(plain(soft, head_part(joined, head, 2)))
        if keep:
            soft_ref[head] = soft
    context = jnp.concatenate(contexts, axis=1).astype(BF16)
    if keep:
        joined_ref[...] = joined
        context_ref[...] = context
    attended = plain(context, output_ref[...])

    @pl.when(step == 0)
    def _():
        total[...] = attended

    @pl.when(step > 0)
    def _():
        total[...] += attended

    @pl.when(step == pl.num_programs(0) - 1)
    def _():
        hidden = x_ref[...].astype(F32) + total[...] + biases_ref[0:1]
        first, normed, inverse = norm_forward(hidden, gains_ref[0:1], biases_ref[1:2])
        first_ref[...] = first
        if keep:
            normed_ref[...] = normed
            inverse_ref[...] = inverse


def units_kernel(keep, first_ref, expand_ref, expand_bias_ref, contract_ref, gains_ref, biases_ref, *rest):
    if keep:
        result_ref, active_ref, slope_ref, normed_ref, inverse_ref, total = rest
    else:
        result_ref, total = rest
    step = pl.program_id(0)
    pre_act = rows_by_units(first_ref[...].astype(BF16), expand_ref[...]) + expand_bias_ref[0]
    cdf = 0.5 * (1.0 + lax.erf(pre_act * 0.5**0.5))
    active = (pre_act * cdf).astype(BF16)
    if keep:
        density = jnp.exp(-0.5 * pre_act * pre_act) * 0.3989422804014327
        slope_ref[...] = (cdf + pre_act * density).astype(BF16)
        active_ref[...] = active
    returned = plain(active, contract_ref[...])

    @pl.when(step == 0)
    def _():
        total[...] = returned

    @pl.when(step > 0)
    def _():
        total[...] += returned

    @pl.when(step == pl.num_programs(0) - 1)
    def _():
        hidden = first_ref[...] + total[...] + biases_ref[2:3]
        result, normed, inverse = norm_forward(hidden, gains_ref[1:2], biases_ref[3:4])
        result_ref[...] = result.astype(BF16)
        if keep:
            normed_ref[...] = normed
            inverse_ref[...] = inverse


def units_back_kernel(
    sums,
    cotangent_ref,
    normed_two_ref,
    inverse_two_ref,
    normed_one_ref,
    inverse_one_ref,
    gains_ref,
    contract_ref,
    expand_ref,
    slope_ref,
    active_ref,
    first_ref,
    *rest,
):
    if sums:
        grad_one_ref, contract_grad_ref, expand_grad_ref, unit_sums_ref, row_sums_ref, returned, total = rest
    else:
        grad_one_ref, returned, total = rest
    step = pl.program_id(0)

    @pl.when(step == 0)
    def _():
        grad_two = norm_backward(
            cotangent_ref[...].astype(F32), normed_two_ref[...], inverse_two_ref[...], gains_ref[1:2]
        )
        returned[...] = grad_two.astype(BF16)
        total[...] = grad_two
        if sums:
            row_sums_ref[4:5] = jnp.sum(grad_two, axis=0, keepdims=True)

    grad_pre = (rows_by_units(returned[...], contract_ref[...]) * slope_ref[...].astype(F32)).astype(BF16)
    total[...] += plain(grad_pre, expand_ref[...])
    if sums:
        contract_grad_ref[...] = over_rows(active_ref[...], returned[...]).astype(BF16)
        expand_grad_ref[...] = over_rows(grad_pre, first_ref[...].astype(BF16)).astype(BF16)
        unit_sums_ref[0] = jnp.sum(grad_pre.astype(F32), axis=0, keepdims=True)

    @pl.when(step == pl.num_programs(0) - 1)
    def _():
        grad_first = total[...]
        normed = normed_one_ref[...]
        grad_one = norm_backward(grad_first, normed, inverse_one_ref[...], gains_ref[0:1])
        grad_one_ref[...] = grad_one
        if sums:
            cotangent = cotangent_ref[...].astype(F32)
            row_sums_ref[0:1] = jnp.sum(grad_first * normed, axis=0, keepdims=True)
            row_sums_ref[1:2] = jnp.sum(cotangent * normed_two_ref[...], axis=0, keepdims=True)
            row_sums_ref[2:3] = jnp.sum(grad_one, axis=0, keepdims=True)
            row_sums_ref[3:4] = jnp.sum(grad_first, axis=0, keepdims=True)
            row_sums_ref[5:6] = jnp.sum(cotangent, axis=0, keepdims=True)


def attention_back_kernel(
    sums, grad_one_ref, output_ref, joined_ref, soft_ref, qkv_ref, x_ref, context_ref, *rest
):
    if sums:
        grad_x_ref, qkv_grad_ref, output_grad_ref, joined_sums_ref, total = rest
    else:
        grad_x_ref, total = rest
    step = pl.program_id(0)

    @pl.when(step == 0)
    def _():
        total[...] = grad_one_ref[...]

    attended = grad_one_ref[...].astype(BF16)
    joined = joined_ref[...]
    grad_context = rows_by_units(attended, output_ref[...]).astype(BF16)
    pieces = []
    for head in range(2):
        grad_head = grad_context[:, head * HD : (head + 1) * HD]
        soft = soft_ref[head]
        soft_float = soft.astype(F32)
        grad_soft = rows_by_units(grad_head, head_part(joined, head, 2))
        inner = jnp.sum(grad_soft * soft_float, axis=-1, keepdims=True)
        grad_scores = (soft_float * (grad_soft - inner)).astype(BF16)
        pieces.append(plain(grad_scores, head_part(joined, head, 1)) * SCALE)
        pieces.append(over_rows(grad_scores, head_part(joined, head, 0)) * SCALE)
        pieces.append(over_rows(soft, grad_head))
    grad_joined = jnp.concatenate(pieces, axis=1).astype(BF16)
    total[...] += plain(grad_joined, qkv_ref[...])
    if sums:
        qkv_grad_ref[...] = over_rows(grad_joined, x_ref[...]).astype(BF16)
        output_grad_ref[...] = over_rows(context_ref[...], attended).astype(BF16)
        joined_sums_ref[0] = jnp.sum(grad_joined.astype(F32), axis=0, keepdims=True)

    @pl.when(step == pl.num_programs(0) - 1)
    def _():
        grad_x_ref[...] = total[...].astype(BF16)


def fixed(*shape):
    return pl.BlockSpec(shape, lambda i: (0,) * len(shape))


def down(rows, columns):
    return pl.BlockSpec((rows, columns), lambda i: (i, 0))


def across(rows, columns):
    return pl.BlockSpec((rows, columns), lambda i: (0, i))


def stacked(count, rows, columns):
    return pl.BlockSpec((count, rows, columns), lambda i: (i, 0, 0))


def shaped(shape, kind):
    return jax.ShapeDtypeStruct(shape, kind)


def run(kernel, steps, in_specs, outs, scratch, flops, args):
    return pl.pallas_call(
        kernel,
        grid=(steps,),
        in_specs=in_specs,
        out_specs=[spec for spec, _ in outs],
        out_shape=[shape for _, shape in outs],
        scratch_shapes=scratch,
        compiler_params=pltpu.CompilerParams(
            vmem_limit_bytes=VMEM_BYTES, dimension_semantics=("arbitrary",)
        ),
        cost_estimate=pl.CostEstimate(flops=flops, bytes_accessed=12_000_000, transcendentals=0),
    )(*args)


def layer_forward(keep, inputs, segment_ids, weights, smalls):
    qkv, output, expand, contract = weights
    qkv_bias, expand_bias, gains, biases = smalls
    rows, features = inputs.shape
    pairs = features // PAIR
    units = expand.shape[0]
    kept = lambda items: items if keep else []
    outs = [(fixed(rows, features), shaped((rows, features), F32))] + kept(
        [
            (across(rows, 3 * PAIR), shaped((rows, 3 * features), BF16)),
            (stacked(2, rows, rows), shaped((2 * pairs, rows, rows), BF16)),
            (across(rows, PAIR), shaped((rows, features), BF16)),
            (fixed(rows, features), shaped((rows, features), F32)),
            (fixed(rows, 1), shaped((rows, 1), F32)),
        ]
    )
    attention = run(
        partial(attention_kernel, keep),
        pairs,
        [
            fixed(rows, features),
            down(3 * PAIR, features),
            stacked(1, 1, 3 * PAIR),
            fixed(rows, 1),
            fixed(1, rows),
            down(PAIR, features),
            fixed(2, features),
            fixed(4, features),
        ],
        outs,
        [pltpu.VMEM((rows, features), F32)],
        8 * rows * features * features + 4 * rows * rows * features,
        (
            inputs,
            qkv,
            qkv_bias.reshape(pairs, 1, 3 * PAIR),
            segment_ids[:, None],
            segment_ids[None, :],
            output,
            gains,
            biases,
        ),
    )
    first = attention[0]
    outs = [(fixed(rows, features), shaped((rows, features), BF16))] + kept(
        [
            (across(rows, CHUNK), shaped((rows, units), BF16)),
            (across(rows, CHUNK), shaped((rows, units), BF16)),
            (fixed(rows, features), shaped((rows, features), F32)),
            (fixed(rows, 1), shaped((rows, 1), F32)),
        ]
    )
    middle = run(
        partial(units_kernel, keep),
        units // CHUNK,
        [
            fixed(rows, features),
            down(CHUNK, features),
            stacked(1, 1, CHUNK),
            down(CHUNK, features),
            fixed(2, features),
            fixed(4, features),
        ],
        outs,
        [pltpu.VMEM((rows, features), F32)],
        4 * rows * features * units,
        (first, expand, expand_bias.reshape(units // CHUNK, 1, CHUNK), contract, gains, biases),
    )
    return (middle[0], (inputs, *attention, *middle[1:]))


def layer_backward(sums, cotangent, weights, gains, saved):
    qkv, output, expand, contract = weights
    inputs, first, joined, soft, context, normed_one, inverse_one, active, slope, normed_two, inverse_two = saved
    rows, features = inputs.shape
    pairs = features // PAIR
    units = expand.shape[0]
    chunks = units // CHUNK
    summed = lambda items: items if sums else []
    whole = fixed(rows, features)
    outs = [(whole, shaped((rows, features), F32))] + summed(
        [
            (down(CHUNK, features), shaped((units, features), BF16)),
            (down(CHUNK, features), shaped((units, features), BF16)),
            (stacked(1, 1, CHUNK), shaped((chunks, 1, CHUNK), F32)),
            (fixed(6, features), shaped((6, features), F32)),
        ]
    )
    middle = run(
        partial(units_back_kernel, sums),
        chunks,
        [
            whole,
            whole,
            fixed(rows, 1),
            whole,
            fixed(rows, 1),
            fixed(2, features),
            down(CHUNK, features),
            down(CHUNK, features),
            across(rows, CHUNK),
            across(rows, CHUNK) if sums else pl.BlockSpec(memory_space=pl.ANY),
            whole if sums else pl.BlockSpec(memory_space=pl.ANY),
        ],
        outs,
        [pltpu.VMEM((rows, features), BF16), pltpu.VMEM((rows, features), F32)],
        (8 if sums else 4) * rows * features * units,
        (
            cotangent,
            normed_two,
            inverse_two,
            normed_one,
            inverse_one,
            gains,
            contract,
            expand,
            slope,
            active,
            first,
        ),
    )
    outs = [(whole, shaped((rows, features), BF16))] + summed(
        [
            (down(3 * PAIR, features), shaped((3 * features, features), BF16)),
            (down(PAIR, features), shaped((features, features), BF16)),
            (stacked(1, 1, 3 * PAIR), shaped((pairs, 1, 3 * PAIR), F32)),
        ]
    )
    attention = run(
        partial(attention_back_kernel, sums),
        pairs,
        [
            whole,
            down(PAIR, features),
            across(rows, 3 * PAIR),
            stacked(2, rows, rows),
            down(3 * PAIR, features),
            whole if sums else pl.BlockSpec(memory_space=pl.ANY),
            across(rows, PAIR) if sums else pl.BlockSpec(memory_space=pl.ANY),
        ],
        outs,
        [pltpu.VMEM((rows, features), F32)],
        (16 if sums else 8) * rows * features * features + 8 * rows * rows * features,
        (middle[0], output, joined, soft, qkv, inputs, context),
    )
    return (attention[0], attention[1:], middle[1:])


def shards(
    ends_in,
    segments,
    qkv_weight,
    qkv_bias,
    output_weight,
    expand_weight,
    expand_bias,
    contract_weight,
    norm_gains,
    row_biases,
):
    section = lax.axis_index("section")
    along = lax.axis_index("tensor")
    dp_count = lax.axis_size("dp")
    tensor_count = lax.axis_size("tensor")
    flat_count = dp_count * tensor_count
    features = ends_in.shape[-1]
    heads = features // HD
    bias_part = qkv_bias.shape[-1]
    unit_part = expand_bias.shape[-1]
    norm_part = norm_gains.shape[-1]
    cut_one = 2 * bias_part
    cut_two = cut_one + unit_part
    cut_three = cut_two + 2 * norm_part
    cut_end = cut_three + 4 * norm_part
    small_rows = -(-cut_end // (16 * features)) * 16
    padding = small_rows * features - cut_end

    packed = jnp.concatenate(
        [
            qkv_bias[0].reshape(-1),
            expand_bias[0],
            norm_gains[0].reshape(-1),
            row_biases[0].reshape(-1),
            jnp.zeros((padding,), BF16),
        ]
    ).reshape(small_rows, features)
    sources = (qkv_weight[0], output_weight[0], expand_weight[0], contract_weight[0], packed)
    gathered = lax.all_gather(jnp.concatenate(sources, axis=0), SHARDS, axis=0, tiled=False)
    own = lax.all_to_all(ends_in[0], "tensor", 0, 1, tiled=True)[0]
    parts = []
    at = 0
    for item in sources:
        parts.append(gathered[:, at : at + item.shape[0]].reshape(-1, features))
        at += item.shape[0]
    weights = tuple(parts[:4])
    packed = parts[4].reshape(flat_count, -1).astype(F32)
    biases_qv = packed[:, :cut_one].reshape(flat_count, 2, bias_part).transpose(1, 0, 2).reshape(2, heads, HD)
    qkv_bias_row = jnp.stack(
        [biases_qv[0], jnp.zeros((heads, HD), F32), biases_qv[1]], axis=1
    ).reshape(-1)
    expand_bias_row = packed[:, cut_one:cut_two].reshape(-1)
    gains = packed[:dp_count, cut_two:cut_three].reshape(dp_count, 2, norm_part).transpose(1, 0, 2).reshape(2, features)
    biases = packed[:dp_count, cut_three:cut_end].reshape(dp_count, 4, norm_part).transpose(1, 0, 2).reshape(4, features)
    smalls = (qkv_bias_row, expand_bias_row, gains, biases)
    segment_ids = lax.dynamic_index_in_dim(segments, along, 0, keepdims=False)[0]

    early_result, _ = layer_forward(False, own, segment_ids, weights, smalls)
    arriving = lax.ppermute(early_result, "section", [(0, 1)])
    inputs = jnp.where(section == 0, own, arriving)
    result, saved = layer_forward(True, inputs, segment_ids, weights, smalls)
    early_grad, _, _ = layer_backward(False, own, weights, gains, saved)
    arriving_grad = lax.ppermute(early_grad, "section", [(1, 0)])
    cotangent = jnp.where(section == 1, own, arriving_grad)
    grad_inputs, attention_grads, unit_grads = layer_backward(True, cotangent, weights, gains, saved)

    joined_sums = attention_grads[2].reshape(heads, 3, HD)
    joined_sums = jnp.stack([joined_sums[:, 0].reshape(-1), joined_sums[:, 2].reshape(-1)])
    norm_sums = unit_grads[3].reshape(6, dp_count, norm_part).transpose(1, 0, 2).reshape(1, dp_count, -1)
    small_grads = jnp.concatenate(
        [
            joined_sums.reshape(2, flat_count, bias_part).transpose(1, 0, 2).reshape(flat_count, -1),
            unit_grads[2].reshape(flat_count, unit_part),
            jnp.broadcast_to(norm_sums, (tensor_count, *norm_sums.shape[1:])).reshape(flat_count, -1),
            jnp.zeros((flat_count, padding), F32),
        ],
        axis=1,
    ).astype(BF16)
    grads = (attention_grads[0], attention_grads[1], unit_grads[1], unit_grads[0], small_grads)
    grads = jnp.concatenate([item.reshape(flat_count, -1, features) for item in grads], axis=1)
    summed = lax.psum_scatter(grads, SHARDS, scatter_dimension=0, tiled=True)[0].astype(F32)
    ends = jnp.where(section == 0, grad_inputs, result).reshape(ends_in.shape[1:])
    ends_out = lax.all_to_all(ends, "tensor", 0, 0, tiled=True).astype(F32)
    results = []
    at = 0
    for item in sources:
        results.append(summed[at : at + item.shape[0]])
        at += item.shape[0]
    small = results[4].reshape(-1)
    return (
        ends_out[None],
        results[0][None],
        small[:cut_one].reshape(1, 2, bias_part),
        results[1][None],
        results[2][None],
        small[None, cut_one:cut_two],
        results[3][None],
        small[cut_two:cut_three].reshape(1, 2, norm_part),
        small[cut_three:cut_end].reshape(1, 4, norm_part),
    )


def solution(mesh):
    rows = P("section", None, ("dp", "tensor"), None)
    units = P("section", SHARDS, None)
    biases = P("section", None, SHARDS)
    norms = P("section", None, "dp")
    vector = P("section", SHARDS)
    return jax.shard_map(
        shards,
        mesh=mesh,
        in_specs=(rows, P(None, "dp", None), units, biases, units, units, vector, units, norms, norms),
        out_specs=(rows, units, biases, units, units, vector, units, norms, norms),
        check_vma=False,
    )
```

```python
from functools import partial

import jax
import jax.numpy as jnp
from jax import lax
from jax.experimental import pallas as pl
from jax.experimental.pallas import tpu as pltpu
from jax.sharding import PartitionSpec as P

HD = 64
EPS = 1e-05
MASKED = -1e30
F32 = jnp.float32
BF16 = jnp.bfloat16
SHARDS = ("tensor", "dp")


def rows_by_units(left_side, right_side):
    return lax.dot_general(
        left_side, right_side, (((1,), (1,)), ((), ())), preferred_element_type=F32
    )


def over_rows(left_side, right_side):
    return lax.dot_general(
        left_side, right_side, (((0,), (0,)), ((), ())), preferred_element_type=F32
    )


def plain(left_side, right_side):
    return jnp.dot(left_side, right_side, preferred_element_type=F32)


def norm_forward(hidden, gain_row, shift_row):
    average = jnp.mean(hidden, axis=-1, keepdims=True)
    centred = hidden - average
    variance = jnp.mean(centred * centred, axis=-1, keepdims=True)
    inverse = lax.rsqrt(variance + EPS)
    normed = centred * inverse
    return (normed * gain_row + shift_row, normed, inverse)


def norm_backward(grad_out, normed, inverse, gain_row):
    grad_normed = grad_out * gain_row
    inner_sum = jnp.mean(grad_normed, axis=-1, keepdims=True)
    along_norm = jnp.mean(grad_normed * normed, axis=-1, keepdims=True)
    return inverse * (grad_normed - inner_sum - normed * along_norm)


SCALE = HD ** (-0.5)
PAIR = 2 * HD
CHUNK = 768
VMEM_BYTES = 50 * 1024 * 1024


def head_part(block, head, part):
    at = (head * 3 + part) * HD
    return block[:, at : at + HD]


def attention_kernel(
    keep, x_ref, qkv_ref, qkv_bias_ref, column_ref, row_ref, output_ref, gains_ref, biases_ref, *rest
):
    if keep:
        first_ref, joined_ref, soft_ref, context_ref, normed_ref, inverse_ref, total = rest
    else:
        first_ref, total = rest
    step = pl.program_id(0)
    joined = (rows_by_units(x_ref[...], qkv_ref[...]) + qkv_bias_ref[0]).astype(BF16)
    same = column_ref[...] == row_ref[...]
    contexts = []
    for head in range(2):
        query = head_part(joined, head, 0) * jnp.asarray(SCALE, BF16)
        scores = jnp.where(same, rows_by_units(query, head_part(joined, head, 1)), MASKED)
        powers = jnp.exp(scores - jnp.max(scores, axis=-1, keepdims=True))
        soft = (powers * (1.0 / jnp.sum(powers, axis=-1, keepdims=True))).astype(BF16)
        contexts.append(plain(soft, head_part(joined, head, 2)))
        if keep:
            soft_ref[head] = soft
    context = jnp.concatenate(contexts, axis=1).astype(BF16)
    if keep:
        joined_ref[...] = joined
        context_ref[...] = context
    attended = plain(context, output_ref[...])

    @pl.when(step == 0)
    def _():
        total[...] = attended

    @pl.when(step > 0)
    def _():
        total[...] += attended

    @pl.when(step == pl.num_programs(0) - 1)
    def _():
        hidden = x_ref[...].astype(F32) + total[...] + biases_ref[0:1]
        first, normed, inverse = norm_forward(hidden, gains_ref[0:1], biases_ref[1:2])
        first_ref[...] = first
        if keep:
            normed_ref[...] = normed
            inverse_ref[...] = inverse


def units_kernel(keep, first_ref, expand_ref, expand_bias_ref, contract_ref, gains_ref, biases_ref, *rest):
    if keep:
        result_ref, active_ref, slope_ref, normed_ref, inverse_ref, total = rest
    else:
        result_ref, total = rest
    step = pl.program_id(0)
    pre_act = rows_by_units(first_ref[...].astype(BF16), expand_ref[...]) + expand_bias_ref[0]
    cdf = 0.5 * (1.0 + lax.erf(pre_act * 0.5**0.5))
    active = (pre_act * cdf).astype(BF16)
    if keep:
        density = jnp.exp(-0.5 * pre_act * pre_act) * 0.3989422804014327
        slope_ref[...] = (cdf + pre_act * density).astype(BF16)
        active_ref[...] = active
    returned = plain(active, contract_ref[...])

    @pl.when(step == 0)
    def _():
        total[...] = returned

    @pl.when(step > 0)
    def _():
        total[...] += returned

    @pl.when(step == pl.num_programs(0) - 1)
    def _():
        hidden = first_ref[...] + total[...] + biases_ref[2:3]
        result, normed, inverse = norm_forward(hidden, gains_ref[1:2], biases_ref[3:4])
        result_ref[...] = result.astype(BF16)
        if keep:
            normed_ref[...] = normed
            inverse_ref[...] = inverse


def units_back_kernel(
    sums,
    cotangent_ref,
    normed_two_ref,
    inverse_two_ref,
    normed_one_ref,
    inverse_one_ref,
    gains_ref,
    contract_ref,
    expand_ref,
    slope_ref,
    active_ref,
    first_ref,
    *rest,
):
    if sums:
        grad_one_ref, contract_grad_ref, expand_grad_ref, unit_sums_ref, row_sums_ref, returned, total = rest
    else:
        grad_one_ref, returned, total = rest
    step = pl.program_id(0)

    @pl.when(step == 0)
    def _():
        grad_two = norm_backward(
            cotangent_ref[...].astype(F32), normed_two_ref[...], inverse_two_ref[...], gains_ref[1:2]
        )
        returned[...] = grad_two.astype(BF16)
        total[...] = grad_two
        if sums:
            row_sums_ref[4:5] = jnp.sum(grad_two, axis=0, keepdims=True)

    grad_pre = (rows_by_units(returned[...], contract_ref[...]) * slope_ref[...].astype(F32)).astype(BF16)
    total[...] += plain(grad_pre, expand_ref[...])
    if sums:
        contract_grad_ref[...] = over_rows(active_ref[...], returned[...]).astype(BF16)
        expand_grad_ref[...] = over_rows(grad_pre, first_ref[...].astype(BF16)).astype(BF16)
        unit_sums_ref[0] = jnp.sum(grad_pre.astype(F32), axis=0, keepdims=True)

    @pl.when(step == pl.num_programs(0) - 1)
    def _():
        grad_first = total[...]
        normed = normed_one_ref[...]
        grad_one = norm_backward(grad_first, normed, inverse_one_ref[...], gains_ref[0:1])
        grad_one_ref[...] = grad_one
        if sums:
            cotangent = cotangent_ref[...].astype(F32)
            row_sums_ref[0:1] = jnp.sum(grad_first * normed, axis=0, keepdims=True)
            row_sums_ref[1:2] = jnp.sum(cotangent * normed_two_ref[...], axis=0, keepdims=True)
            row_sums_ref[2:3] = jnp.sum(grad_one, axis=0, keepdims=True)
            row_sums_ref[3:4] = jnp.sum(grad_first, axis=0, keepdims=True)
            row_sums_ref[5:6] = jnp.sum(cotangent, axis=0, keepdims=True)


def attention_back_kernel(
    sums, grad_one_ref, output_ref, joined_ref, soft_ref, qkv_ref, x_ref, context_ref, *rest
):
    if sums:
        grad_x_ref, qkv_grad_ref, output_grad_ref, joined_sums_ref, total = rest
    else:
        grad_x_ref, total = rest
    step = pl.program_id(0)

    @pl.when(step == 0)
    def _():
        total[...] = grad_one_ref[...]

    attended = grad_one_ref[...].astype(BF16)
    joined = joined_ref[...]
    grad_context = rows_by_units(attended, output_ref[...]).astype(BF16)
    pieces = []
    for head in range(2):
        grad_head = grad_context[:, head * HD : (head + 1) * HD]
        soft = soft_ref[head]
        soft_float = soft.astype(F32)
        grad_soft = rows_by_units(grad_head, head_part(joined, head, 2))
        inner = jnp.sum(grad_soft * soft_float, axis=-1, keepdims=True)
        grad_scores = (soft_float * (grad_soft - inner)).astype(BF16)
        pieces.append(plain(grad_scores, head_part(joined, head, 1)) * SCALE)
        pieces.append(over_rows(grad_scores, head_part(joined, head, 0)) * SCALE)
        pieces.append(over_rows(soft, grad_head))
    grad_joined = jnp.concatenate(pieces, axis=1).astype(BF16)
    total[...] += plain(grad_joined, qkv_ref[...])
    if sums:
        qkv_grad_ref[...] = over_rows(grad_joined, x_ref[...]).astype(BF16)
        output_grad_ref[...] = over_rows(context_ref[...], attended).astype(BF16)
        joined_sums_ref[0] = jnp.sum(grad_joined.astype(F32), axis=0, keepdims=True)

    @pl.when(step == pl.num_programs(0) - 1)
    def _():
        grad_x_ref[...] = total[...].astype(BF16)


def fixed(*shape):
    return pl.BlockSpec(shape, lambda i: (0,) * len(shape))


def down(rows, columns):
    return pl.BlockSpec((rows, columns), lambda i: (i, 0))


def across(rows, columns):
    return pl.BlockSpec((rows, columns), lambda i: (0, i))


def stacked(count, rows, columns):
    return pl.BlockSpec((count, rows, columns), lambda i: (i, 0, 0))


def shaped(shape, kind):
    return jax.ShapeDtypeStruct(shape, kind)


def run(kernel, steps, in_specs, outs, scratch, flops, args):
    return pl.pallas_call(
        kernel,
        grid=(steps,),
        in_specs=in_specs,
        out_specs=[spec for spec, _ in outs],
        out_shape=[shape for _, shape in outs],
        scratch_shapes=scratch,
        compiler_params=pltpu.CompilerParams(
            vmem_limit_bytes=VMEM_BYTES, dimension_semantics=("arbitrary",)
        ),
        cost_estimate=pl.CostEstimate(flops=flops, bytes_accessed=12_000_000, transcendentals=0),
    )(*args)


def layer_forward(keep, inputs, segment_ids, weights, smalls):
    qkv, output, expand, contract = weights
    qkv_bias, expand_bias, gains, biases = smalls
    rows, features = inputs.shape
    pairs = features // PAIR
    units = expand.shape[0]
    kept = lambda items: items if keep else []
    outs = [(fixed(rows, features), shaped((rows, features), F32))] + kept(
        [
            (across(rows, 3 * PAIR), shaped((rows, 3 * features), BF16)),
            (stacked(2, rows, rows), shaped((2 * pairs, rows, rows), BF16)),
            (across(rows, PAIR), shaped((rows, features), BF16)),
            (fixed(rows, features), shaped((rows, features), F32)),
            (fixed(rows, 1), shaped((rows, 1), F32)),
        ]
    )
    attention = run(
        partial(attention_kernel, keep),
        pairs,
        [
            fixed(rows, features),
            down(3 * PAIR, features),
            stacked(1, 1, 3 * PAIR),
            fixed(rows, 1),
            fixed(1, rows),
            down(PAIR, features),
            fixed(2, features),
            fixed(4, features),
        ],
        outs,
        [pltpu.VMEM((rows, features), F32)],
        8 * rows * features * features + 4 * rows * rows * features,
        (
            inputs,
            qkv,
            qkv_bias.reshape(pairs, 1, 3 * PAIR),
            segment_ids[:, None],
            segment_ids[None, :],
            output,
            gains,
            biases,
        ),
    )
    first = attention[0]
    outs = [(fixed(rows, features), shaped((rows, features), BF16))] + kept(
        [
            (across(rows, CHUNK), shaped((rows, units), BF16)),
            (across(rows, CHUNK), shaped((rows, units), BF16)),
            (fixed(rows, features), shaped((rows, features), F32)),
            (fixed(rows, 1), shaped((rows, 1), F32)),
        ]
    )
    middle = run(
        partial(units_kernel, keep),
        units // CHUNK,
        [
            fixed(rows, features),
            down(CHUNK, features),
            stacked(1, 1, CHUNK),
            down(CHUNK, features),
            fixed(2, features),
            fixed(4, features),
        ],
        outs,
        [pltpu.VMEM((rows, features), F32)],
        4 * rows * features * units,
        (first, expand, expand_bias.reshape(units // CHUNK, 1, CHUNK), contract, gains, biases),
    )
    return (middle[0], (inputs, *attention, *middle[1:]))


def layer_backward(sums, cotangent, weights, gains, saved):
    qkv, output, expand, contract = weights
    inputs, first, joined, soft, context, normed_one, inverse_one, active, slope, normed_two, inverse_two = saved
    rows, features = inputs.shape
    pairs = features // PAIR
    units = expand.shape[0]
    chunks = units // CHUNK
    summed = lambda items: items if sums else []
    whole = fixed(rows, features)
    outs = [(whole, shaped((rows, features), F32))] + summed(
        [
            (down(CHUNK, features), shaped((units, features), BF16)),
            (down(CHUNK, features), shaped((units, features), BF16)),
            (stacked(1, 1, CHUNK), shaped((chunks, 1, CHUNK), F32)),
            (fixed(6, features), shaped((6, features), F32)),
        ]
    )
    middle = run(
        partial(units_back_kernel, sums),
        chunks,
        [
            whole,
            whole,
            fixed(rows, 1),
            whole,
            fixed(rows, 1),
            fixed(2, features),
            down(CHUNK, features),
            down(CHUNK, features),
            across(rows, CHUNK),
            across(rows, CHUNK) if sums else pl.BlockSpec(memory_space=pl.ANY),
            whole if sums else pl.BlockSpec(memory_space=pl.ANY),
        ],
        outs,
        [pltpu.VMEM((rows, features), BF16), pltpu.VMEM((rows, features), F32)],
        (8 if sums else 4) * rows * features * units,
        (
            cotangent,
            normed_two,
            inverse_two,
            normed_one,
            inverse_one,
            gains,
            contract,
            expand,
            slope,
            active,
            first,
        ),
    )
    outs = [(whole, shaped((rows, features), BF16))] + summed(
        [
            (down(3 * PAIR, features), shaped((3 * features, features), BF16)),
            (down(PAIR, features), shaped((features, features), BF16)),
            (stacked(1, 1, 3 * PAIR), shaped((pairs, 1, 3 * PAIR), F32)),
        ]
    )
    attention = run(
        partial(attention_back_kernel, sums),
        pairs,
        [
            whole,
            down(PAIR, features),
            across(rows, 3 * PAIR),
            stacked(2, rows, rows),
            down(3 * PAIR, features),
            whole if sums else pl.BlockSpec(memory_space=pl.ANY),
            across(rows, PAIR) if sums else pl.BlockSpec(memory_space=pl.ANY),
        ],
        outs,
        [pltpu.VMEM((rows, features), F32)],
        (16 if sums else 8) * rows * features * features + 8 * rows * rows * features,
        (middle[0], output, joined, soft, qkv, inputs, context),
    )
    return (attention[0], attention[1:], middle[1:])


def shards(
    ends_in,
    segments,
    qkv_weight,
    qkv_bias,
    output_weight,
    expand_weight,
    expand_bias,
    contract_weight,
    norm_gains,
    row_biases,
):
    section = lax.axis_index("section")
    along = lax.axis_index("tensor")
    dp_count = lax.axis_size("dp")
    tensor_count = lax.axis_size("tensor")
    flat_count = dp_count * tensor_count
    features = ends_in.shape[-1]
    heads = features // HD
    bias_part = qkv_bias.shape[-1]
    unit_part = expand_bias.shape[-1]
    norm_part = norm_gains.shape[-1]
    cut_one = 2 * bias_part
    cut_two = cut_one + unit_part
    cut_three = cut_two + 2 * norm_part
    cut_end = cut_three + 4 * norm_part
    small_rows = -(-cut_end // (16 * features)) * 16
    padding = small_rows * features - cut_end

    packed = jnp.concatenate(
        [
            qkv_bias[0].reshape(-1),
            expand_bias[0],
            norm_gains[0].reshape(-1),
            row_biases[0].reshape(-1),
            jnp.zeros((padding,), BF16),
        ]
    ).reshape(small_rows, features)
    sources = (qkv_weight[0], output_weight[0], expand_weight[0], contract_weight[0], packed)
    early_sources = (qkv_weight[0], output_weight[0], packed)
    late_sources = (expand_weight[0], contract_weight[0])
    early = lax.all_gather(jnp.concatenate(early_sources, axis=0), SHARDS, axis=0, tiled=False)
    late_block = jnp.concatenate(late_sources, axis=0)
    own = lax.all_to_all(ends_in[0], "tensor", 0, 1, tiled=True)[0]
    early, late_block, own = lax.optimization_barrier((early, late_block, own))
    late = lax.all_gather(late_block, SHARDS, axis=0, tiled=False)
    parts = []
    for block, items in ((early, early_sources), (late, late_sources)):
        at = 0
        for item in items:
            parts.append(block[:, at : at + item.shape[0]].reshape(-1, features))
            at += item.shape[0]
    weights = (parts[0], parts[1], parts[3], parts[4])
    packed = parts[2].reshape(flat_count, -1).astype(F32)
    biases_qv = packed[:, :cut_one].reshape(flat_count, 2, bias_part).transpose(1, 0, 2).reshape(2, heads, HD)
    qkv_bias_row = jnp.stack(
        [biases_qv[0], jnp.zeros((heads, HD), F32), biases_qv[1]], axis=1
    ).reshape(-1)
    expand_bias_row = packed[:, cut_one:cut_two].reshape(-1)
    gains = packed[:dp_count, cut_two:cut_three].reshape(dp_count, 2, norm_part).transpose(1, 0, 2).reshape(2, features)
    biases = packed[:dp_count, cut_three:cut_end].reshape(dp_count, 4, norm_part).transpose(1, 0, 2).reshape(4, features)
    smalls = (qkv_bias_row, expand_bias_row, gains, biases)
    segment_ids = lax.dynamic_index_in_dim(segments, along, 0, keepdims=False)[0]

    early_result, _ = layer_forward(False, own, segment_ids, weights, smalls)
    arriving = lax.ppermute(early_result, "section", [(0, 1)])
    inputs = jnp.where(section == 0, own, arriving)
    result, saved = layer_forward(True, inputs, segment_ids, weights, smalls)
    early_grad, _, _ = layer_backward(False, own, weights, gains, saved)
    arriving_grad = lax.ppermute(early_grad, "section", [(1, 0)])
    cotangent = jnp.where(section == 1, own, arriving_grad)
    grad_inputs, attention_grads, unit_grads = layer_backward(True, cotangent, weights, gains, saved)

    joined_sums = attention_grads[2].reshape(heads, 3, HD)
    joined_sums = jnp.stack([joined_sums[:, 0].reshape(-1), joined_sums[:, 2].reshape(-1)])
    norm_sums = unit_grads[3].reshape(6, dp_count, norm_part).transpose(1, 0, 2).reshape(1, dp_count, -1)
    small_grads = jnp.concatenate(
        [
            joined_sums.reshape(2, flat_count, bias_part).transpose(1, 0, 2).reshape(flat_count, -1),
            unit_grads[2].reshape(flat_count, unit_part),
            jnp.broadcast_to(norm_sums, (tensor_count, *norm_sums.shape[1:])).reshape(flat_count, -1),
            jnp.zeros((flat_count, padding), F32),
        ],
        axis=1,
    ).astype(BF16)
    grads = (attention_grads[0], attention_grads[1], unit_grads[1], unit_grads[0], small_grads)
    grads = jnp.concatenate([item.reshape(flat_count, -1, features) for item in grads], axis=1)
    summed = lax.psum_scatter(grads, SHARDS, scatter_dimension=0, tiled=True)[0].astype(F32)
    ends = jnp.where(section == 0, grad_inputs, result).reshape(ends_in.shape[1:])
    ends_out = lax.all_to_all(ends, "tensor", 0, 0, tiled=True).astype(F32)
    results = []
    at = 0
    for item in sources:
        results.append(summed[at : at + item.shape[0]])
        at += item.shape[0]
    small = results[4].reshape(-1)
    return (
        ends_out[None],
        results[0][None],
        small[:cut_one].reshape(1, 2, bias_part),
        results[1][None],
        results[2][None],
        small[None, cut_one:cut_two],
        results[3][None],
        small[cut_two:cut_three].reshape(1, 2, norm_part),
        small[cut_three:cut_end].reshape(1, 4, norm_part),
    )


def solution(mesh):
    rows = P("section", None, ("dp", "tensor"), None)
    units = P("section", SHARDS, None)
    biases = P("section", None, SHARDS)
    norms = P("section", None, "dp")
    vector = P("section", SHARDS)
    return jax.shard_map(
        shards,
        mesh=mesh,
        in_specs=(rows, P(None, "dp", None), units, biases, units, units, vector, units, norms, norms),
        out_specs=(rows, units, biases, units, units, vector, units, norms, norms),
        check_vma=False,
    )
```
